32 devices in a mesh: chan: 16 (over z, x, core), day: 2 (over y).
Axes of the slice: x: 2, y: 2, z: 4, core: 2. Of those that a mesh axis runs over, the one named last changes fastest.
Arguments:
- spectra: bfloat16 [2, 256, 2, 4096], P('day', 'chan'), may hold values from -6 to 6
- source_index: int32 [16], replicated, may hold values from 0 to 255, as said below
- interrogator: int32 [256], P('chan'), may hold values from 0 to 7, as said below
- lag_bounds: int32 [16, 2], replicated, may hold values from 0 to 256, as said below
Outputs:
- reference_stack: bfloat16 [16, 256, 256], P('day', 'chan')
- drift: float32 [2, 8], P('day')
The draws below stay inside these ranges and needn't reach their ends.
Inputs may be any that keep to these rules, and one draw needn't show every extreme that they name: `source_index`: distinct channels. Each interrogator serves one contiguous run of channels, in rising order, of at least 16 channels. `lag_bounds`: first lag below end lag, and each window spans at least 128 lags.
All inputs are finite; a program needn't handle non-finite values.
Results may differ from the reference program's by a relative error of at most 0.0065.
Values may be sent and summed in bfloat16 or wider, within the bound.
A program may use at most 64 MiB of HBM per device.

```python
import math
import jax
import jax.numpy as jnp
from jax import lax

BINS = 4096
LAGS = 256
NSRC = 16
NINT = 8
CHANNELS = 256
DAYS = 2


def draw_source_index(key, part):
    return jax.random.permutation(jax.random.fold_in(key, 11), CHANNELS)[:NSRC].astype(jnp.int32)


def draw_interrogator(key, part):
    span = CHANNELS // NINT
    jitter = CHANNELS // (4 * NINT)
    steps = jnp.arange(1, NINT, dtype=jnp.int32)
    cuts = steps * span + jax.random.randint(jax.random.fold_in(key, 23), (NINT - 1,), -jitter, jitter + 1)
    channel = jnp.arange(CHANNELS, dtype=jnp.int32)
    return jnp.sum((channel[:, None] >= cuts[None, :]).astype(jnp.int32), 1).astype(jnp.int32)


def draw_lag_bounds(key, part):
    first = jax.random.randint(jax.random.fold_in(key, 31), (NSRC,), 0, LAGS // 4)
    last = LAGS - jax.random.randint(jax.random.fold_in(key, 37), (NSRC,), 0, LAGS // 4)
    first = first.at[0].set(0)
    last = last.at[0].set(LAGS)
    return jnp.stack([first, last], 1).astype(jnp.int32)


def shard_levels(own_key, shape, pieces, low, largest):
    def one(dim, blocks):
        heights = jax.random.uniform(jax.random.fold_in(jax.random.fold_in(own_key, 6), dim), (blocks,), jnp.float32, low / len(pieces), largest / len(pieces))
        return jnp.repeat(jnp.exp(heights), shape[dim] // blocks).reshape((-1,) + (1,) * (len(shape) - dim - 1))

    gain = one(*pieces[0])
    for cut in pieces[1:]:
        gain = gain * one(*cut)
    return gain


def bell_draw(rng, dims, width, limit, pieces=(), held_as=jnp.bfloat16):
    factor_of = shard_levels(rng, dims, pieces, -0.22, 0.18) if pieces else 1.0
    drawn = jax.random.normal(rng, dims, jnp.float32) * width * factor_of
    return jnp.minimum(jnp.maximum(drawn, -limit), limit).astype(held_as)


def setup_inputs(seed: int = 0) -> dict:
    streams_of = jax.random.split(jax.random.key(seed), 5)
    spectra = bell_draw(streams_of[0], (DAYS, CHANNELS, 2, BINS), 1.0, 6.0, ((0, 2), (1, 16)))
    source_index = draw_source_index(jax.random.fold_in(streams_of[4], 71), 0)
    interrogator = draw_interrogator(jax.random.fold_in(streams_of[4], 71), 0)
    lag_bounds = draw_lag_bounds(jax.random.fold_in(streams_of[4], 71), 0)
    return dict(spectra=spectra, source_index=source_index, interrogator=interrogator, lag_bounds=lag_bounds)


def lag_table(bins, lags):
    freq = jnp.arange(bins, dtype=jnp.int32)
    shift = jnp.arange(lags, dtype=jnp.int32) - lags // 2
    phase = freq[:, None] * shift[None, :] % (2 * bins)
    angle = math.pi * phase.astype(jnp.float32) / bins
    scale = 1.0 / math.sqrt(bins)
    return jnp.concatenate([jnp.cos(angle) * scale, -jnp.sin(angle) * scale], 0).astype(jnp.bfloat16)

def correlate(spec_day, source, table):
    local = spec_day.astype(jnp.float32)
    chosen = source.astype(jnp.float32)
    real_in, imag_in = (local[:, 0], local[:, 1])
    real_src, imag_src = (chosen[0][None, :], chosen[1][None, :])
    cross = jnp.concatenate([real_in * real_src + imag_in * imag_src, imag_in * real_src - real_in * imag_src], -1).astype(jnp.bfloat16)
    return jnp.dot(cross, table, preferred_element_type=jnp.float32)

def reference(spectra, source_index, interrogator, lag_bounds):
    table = lag_table(BINS, LAGS)

    def one_day(carry, spec_day):
        sources = spec_day[source_index]
        corr = lax.map(lambda source: correlate(spec_day, source, table), sources)
        return (carry + corr, corr)
    total, corr_all = lax.scan(one_day, jnp.zeros((NSRC, CHANNELS, LAGS), jnp.float32), spectra)
    reference_stack = (total / DAYS).astype(jnp.bfloat16)
    ref_float = reference_stack.astype(jnp.float32)
    lag_pos = jnp.arange(LAGS, dtype=jnp.int32)
    window = ((lag_pos[None, :] >= lag_bounds[:, 0:1]) & (lag_pos[None, :] < lag_bounds[:, 1:2])).astype(jnp.float32)
    member = (interrogator[:, None] == jnp.arange(NINT, dtype=jnp.int32)[None, :]).astype(jnp.float32)

    def drift_day(corr):
        padded = jnp.pad(corr, ((0, 0), (0, 0), (1, 1)))
        slope = 0.5 * (padded[:, :, 2:] - padded[:, :, :-2])
        weighted = window[:, None, :] * slope
        num_chan = lax.optimization_barrier(jnp.sum(weighted * (corr - ref_float), axis=(0, 2)))
        den_chan = lax.optimization_barrier(jnp.sum(weighted * slope, axis=(0, 2)))
        num = lax.optimization_barrier(jnp.sum(num_chan[:, None] * member, 0))
        den = lax.optimization_barrier(jnp.sum(den_chan[:, None] * member, 0))
        return num / (den + 1e-06)
    drift = lax.map(drift_day, corr_all)
    return (reference_stack, drift)
```

```python
import functools
import math

import jax
import jax.numpy as jnp
import numpy as np
from jax import lax
from jax.experimental import pallas as pl
from jax.experimental.pallas import tpu as pltpu
from jax.sharding import PartitionSpec as P

LAGS = 256
NINT = 8
LANES = 128
MESH = pl.DeviceIdType.MESH


def lag_table(bins, lags):
    freq = np.arange(bins, dtype=np.int32)
    shift = np.arange(lags, dtype=np.int32) - lags // 2
    phase = freq[:, None] * shift[None, :] % (2 * bins)
    angle = np.float32(math.pi) * phase.astype(np.float32) / np.float32(bins)
    scale = np.float32(1.0 / math.sqrt(bins))
    return np.stack([np.cos(angle) * scale, -np.sin(angle) * scale]).astype(jnp.bfloat16)


def column(row):
    m = row.shape[1]
    wide = jnp.broadcast_to(row.astype(jnp.float32), (m, m))
    eye = lax.broadcasted_iota(jnp.int32, (m, m), 0) == lax.broadcasted_iota(jnp.int32, (m, m), 1)
    return jnp.sum(jnp.where(eye, wide, 0.0), axis=1, keepdims=True)


def kernel(
    n, days, bounds_ref, index_ref, inter_ref, local_ref, table_hbm, ref_out, drift_out,
    table, mine, parts, gath, cross, acc, day_send, day_recv, fit,
    table_sem, rs_send, rs_recv, ag_send, ag_recv, dy_send, dy_recv, ft_send, ft_recv,
):
    me = lax.axis_index("chan")
    today = lax.axis_index("day")
    ch = local_ref.shape[2]
    nsrc = mine.shape[2]
    chunk = mine.shape[3]
    share = nsrc // days
    rows = share * ch

    load = pltpu.make_async_copy(table_hbm, table, table_sem)
    load.start()

    barrier = pltpu.get_barrier_semaphore()

    def greet(step, carry):
        c = lax.rem(me + lax.rem(step, n), n)
        d = lax.rem(today + step // n, days)
        pl.semaphore_signal(barrier, inc=1, device_id={"chan": c, "day": d}, device_id_type=MESH)
        return carry

    lax.fori_loop(1, n * days, greet, 0)

    wanted = column(index_ref[...]) - (me * ch).astype(jnp.float32)
    select = (
        wanted == lax.broadcasted_iota(jnp.int32, (nsrc, ch), 1).astype(jnp.float32)
    ).astype(jnp.bfloat16)

    def pick(j, carry):
        for part in range(2):
            mine[j, part] = jnp.dot(
                select, local_ref[j, part], preferred_element_type=jnp.float32
            ).astype(jnp.bfloat16)
        return carry

    lax.fori_loop(0, n, pick, 0)
    pl.semaphore_wait(barrier, n * days - 1)

    def scatter(k):
        peer = lax.rem(me + k, n)
        return pltpu.make_async_remote_copy(
            src_ref=mine.at[peer], dst_ref=parts.at[k], send_sem=rs_send.at[k],
            recv_sem=rs_recv.at[k], device_id={"chan": peer}, device_id_type=MESH,
        )

    def gather(k):
        peer = lax.rem(me + k, n)
        return pltpu.make_async_remote_copy(
            src_ref=gath.at[0], dst_ref=gath.at[k], send_sem=ag_send.at[k],
            recv_sem=ag_recv.at[k], device_id={"chan": peer}, device_id_type=MESH,
        )

    for k in range(1, n):
        scatter(k).start()
    own = mine[me].astype(jnp.float32)
    for k in range(1, n):
        scatter(k).wait_recv()
        own = own + parts[k].astype(jnp.float32)
    gath[0] = own.astype(jnp.bfloat16)
    for k in range(1, n):
        gather(k).start()
    load.wait()

    def correlate(k):
        j = lax.rem(me - k + n, n)
        sr = local_ref[j, 0].astype(jnp.float32)
        si = local_ref[j, 1].astype(jnp.float32)
        vr = gath[k, 0].astype(jnp.float32)
        vi = gath[k, 1].astype(jnp.float32)
        for s in range(nsrc):
            ar, ai = vr[s : s + 1], vi[s : s + 1]
            at = pl.ds(s * ch, ch)
            cross[at, :chunk] = (sr * ar + si * ai).astype(jnp.bfloat16)
            cross[at, chunk:] = (si * ar - sr * ai).astype(jnp.bfloat16)
        return jnp.dot(cross[...], table[j], preferred_element_type=jnp.float32)

    acc[...] = correlate(0)

    def step(k, carry):
        gather(k).wait_recv()
        acc[...] += correlate(k)
        return carry

    lax.fori_loop(1, n, step, 0)

    def exchange(k):
        peer = lax.rem(today + k, days)
        return pltpu.make_async_remote_copy(
            src_ref=day_send.at[peer], dst_ref=day_recv.at[k], send_sem=dy_send.at[k],
            recv_sem=dy_recv.at[k], device_id={"day": peer}, device_id_type=MESH,
        )

    for d in range(days):
        day_send[d] = acc[d * rows : (d + 1) * rows].astype(jnp.bfloat16)
    for k in range(1, days):
        exchange(k).start()

    def finish(kc, kd):
        at = kd * n + kc
        return pltpu.make_async_remote_copy(
            src_ref=fit.at[n * days + kd], dst_ref=fit.at[at], send_sem=ft_send.at[at],
            recv_sem=ft_recv.at[at],
            device_id={"chan": lax.rem(me + kc, n), "day": lax.rem(today - kd + days, days)},
            device_id_type=MESH,
        )

    lag = lax.broadcasted_iota(jnp.int32, (ch, LAGS), 1)
    member = (
        column(inter_ref[...]) == lax.broadcasted_iota(jnp.int32, (ch, LANES), 1).astype(jnp.float32)
    ).astype(jnp.float32)
    late = (
        column(inter_ref[...]) + LANES // 2
        == lax.broadcasted_iota(jnp.int32, (ch, LANES), 1).astype(jnp.float32)
    ).astype(jnp.float32)
    base = today * rows
    for k in range(1, days):
        exchange(k).wait_recv()
    nums = [jnp.zeros((ch, LAGS), jnp.float32) for _ in range(days)]
    dens = [jnp.zeros((ch, LAGS), jnp.float32) for _ in range(days)]
    for s in range(share):
        corrs = [acc[pl.ds(pl.multiple_of(base + s * ch, ch), ch)]]
        for k in range(1, days):
            corrs.append(day_recv[k, s * ch : (s + 1) * ch].astype(jnp.float32))
        mean = (sum(corrs[1:], corrs[0]) / days).astype(jnp.bfloat16)
        ref_out[s] = mean
        mean = mean.astype(jnp.float32)
        lo = bounds_ref[today * share + s, 0]
        hi = bounds_ref[today * share + s, 1]
        inside = (lag >= lo) & (lag < hi)
        for k in range(days):
            after = jnp.where(lag == LAGS - 1, 0.0, pltpu.roll(corrs[k], LAGS - 1, 1))
            before = jnp.where(lag == 0, 0.0, pltpu.roll(corrs[k], 1, 1))
            slope = 0.5 * (after - before)
            weighted = jnp.where(inside, slope, 0.0)
            nums[k] = nums[k] + weighted * (corrs[k] - mean)
            dens[k] = dens[k] + weighted * slope
    for k in range(days):
        num = jnp.sum(nums[k], axis=1, keepdims=True)
        den = jnp.sum(dens[k], axis=1, keepdims=True)
        fit[n * days + k] = jnp.sum(num * member + den * late, axis=0, keepdims=True)
    for kd in range(days):
        def send(kc, carry, kd=kd):
            finish(kc, kd).start()
            return carry

        lax.fori_loop(1 if kd == 0 else 0, n, send, 0)
    total = fit[n * days]

    def collect(at, total):
        finish(lax.rem(at, n), at // n).wait_recv()
        return total + fit[at]

    total = lax.fori_loop(1, n * days, collect, total)
    drift_out[...] = (total / (pltpu.roll(total, LANES // 2, 1) + 1e-06))[:, :NINT]

    for k in range(1, n):
        scatter(k).wait_send()
        gather(k).wait_send()
    for k in range(1, days):
        exchange(k).wait_send()

    def drain(at, carry):
        finish(lax.rem(at, n), at // n).wait_send()
        return carry

    lax.fori_loop(1, n * days, drain, 0)


def per_device(n, days, spectra, source_index, interrogator, lag_bounds):
    _, ch, _, bins = spectra.shape
    nsrc = source_index.shape[0]
    chunk = bins // n
    share = nsrc // days
    table = lag_table(bins, LAGS).reshape(2, n, chunk, LAGS).transpose(1, 0, 2, 3)
    table = jnp.asarray(table.reshape(n, 2 * chunk, LAGS))
    local = spectra[0].reshape(ch, 2, n, chunk).transpose(2, 1, 0, 3)
    vmem = pl.BlockSpec(memory_space=pltpu.VMEM)
    dma = pltpu.SemaphoreType.DMA
    bf16, f32 = jnp.bfloat16, jnp.float32
    ref_out, drift = pl.pallas_call(
        functools.partial(kernel, n, days),
        out_shape=(
            jax.ShapeDtypeStruct((share, ch, LAGS), bf16),
            jax.ShapeDtypeStruct((1, NINT), f32),
        ),
        in_specs=[
            pl.BlockSpec(memory_space=pltpu.SMEM), vmem, vmem, vmem,
            pl.BlockSpec(memory_space=pl.ANY),
        ],
        out_specs=(vmem, vmem),
        scratch_shapes=[
            pltpu.VMEM((n, 2 * chunk, LAGS), bf16),
            pltpu.VMEM((n, 2, nsrc, chunk), bf16),
            pltpu.VMEM((n, 2, nsrc, chunk), bf16),
            pltpu.VMEM((n, 2, nsrc, chunk), bf16),
            pltpu.VMEM((nsrc * ch, 2 * chunk), bf16),
            pltpu.VMEM((nsrc * ch, LAGS), f32),
            pltpu.VMEM((days, share * ch, LAGS), bf16),
            pltpu.VMEM((days, share * ch, LAGS), bf16),
            pltpu.VMEM((n * days + days, 1, LANES), f32),
            dma, dma((n,)), dma((n,)), dma((n,)), dma((n,)), dma((days,)), dma((days,)),
            dma((n * days,)), dma((n * days,)),
        ],
        compiler_params=pltpu.CompilerParams(
            collective_id=0, has_side_effects=True, vmem_limit_bytes=32 * 1024 * 1024
        ),
    )(lag_bounds, source_index[None], interrogator[None], local, table)
    return ref_out, drift


def solution(mesh):
    return jax.shard_map(
        functools.partial(per_device, mesh.shape["chan"], mesh.shape["day"]),
        mesh=mesh,
        in_specs=(P("day", "chan", None, None), P(), P("chan"), P()),
        out_specs=(P("day", "chan", None), P("day", None)),
        check_vma=False,
    )
```

```python
import functools
import math

import jax
import jax.numpy as jnp
import numpy as np
from jax import lax
from jax.experimental import pallas as pl
from jax.experimental.pallas import tpu as pltpu
from jax.sharding import PartitionSpec as P

LAGS = 256
NINT = 8
LANES = 128
MESH = pl.DeviceIdType.MESH


def lag_table(bins, lags):
    freq = np.arange(bins, dtype=np.int32)
    shift = np.arange(lags, dtype=np.int32) - lags // 2
    phase = freq[:, None] * shift[None, :] % (2 * bins)
    angle = np.float32(math.pi) * phase.astype(np.float32) / np.float32(bins)
    scale = np.float32(1.0 / math.sqrt(bins))
    return np.stack([np.cos(angle) * scale, -np.sin(angle) * scale]).astype(jnp.bfloat16)


def column(row):
    m = row.shape[1]
    wide = jnp.broadcast_to(row.astype(jnp.float32), (m, m))
    eye = lax.broadcasted_iota(jnp.int32, (m, m), 0) == lax.broadcasted_iota(jnp.int32, (m, m), 1)
    return jnp.sum(jnp.where(eye, wide, 0.0), axis=1, keepdims=True)


def kernel(
    outers, inners, days, bounds_hbm, index_hbm, inter_hbm, local_hbm, table_hbm, ref_out, drift_out,
    bounds_ref, index_ref, inter_ref, local_ref, window, table, mine, parts, half, parts2, gath, cross, acc, day_send, day_recv, fit,
    in_sem, table_sem, rs_send, rs_recv, rt_send, rt_recv, ag_send, ag_recv, fw_send, fw_recv,
    dy_send, dy_recv, fp_send, fp_recv, ft_send, ft_recv,
):
    n = outers * inners
    me = lax.axis_index("chan")
    outer, inner = me // inners, lax.rem(me, inners)
    today = lax.axis_index("day")
    ch = local_ref.shape[2]
    nsrc = mine.shape[3]
    chunk = mine.shape[4]
    share = nsrc // days
    rows = share * ch

    load = pltpu.make_async_copy(table_hbm, table, table_sem)
    ins = [
        pltpu.make_async_copy(src, dst, in_sem.at[i])
        for i, (src, dst) in enumerate([
            (index_hbm, index_ref), (local_hbm, local_ref),
            (inter_hbm, inter_ref), (bounds_hbm, bounds_ref),
        ])
    ]
    for copy in ins:
        copy.start()
    load.start()

    barrier = pltpu.get_barrier_semaphore()

    def along(o, i, d):
        chan = lax.rem(outer + o, outers) * inners + lax.rem(inner + i, inners)
        return {"chan": chan, "day": lax.rem(today + d, days)}

    partners = [(o, 0, 0) for o in range(1, outers)]
    partners += [(0, i, d) for d in range(days) for i in range(inners) if i or d]
    for partner in partners:
        pl.semaphore_signal(barrier, inc=1, device_id=along(*partner), device_id_type=MESH)

    for copy in ins:
        copy.wait()

    wanted = column(index_ref[...]) - (me * ch).astype(jnp.float32)
    select = (
        wanted == lax.broadcasted_iota(jnp.int32, (nsrc, ch), 1).astype(jnp.float32)
    ).astype(jnp.bfloat16)

    for i in range(inners):
        for o in range(outers):
            for part in range(2):
                mine[i, o, part] = jnp.dot(
                    select, local_ref[o * inners + i, part], preferred_element_type=jnp.float32
                ).astype(jnp.bfloat16)
    pl.semaphore_wait(barrier, len(partners))

    def remote(src, dst, send_sem, recv_sem, to):
        return pltpu.make_async_remote_copy(
            src_ref=src, dst_ref=dst, send_sem=send_sem, recv_sem=recv_sem,
            device_id=along(*to), device_id_type=MESH,
        )

    scatter = [
        remote(mine.at[lax.rem(inner + i, inners)], parts.at[i], rs_send.at[i], rs_recv.at[i], (0, i, 0))
        for i in range(1, inners)
    ]
    across = [
        remote(half.at[lax.rem(outer + o, outers)], parts2.at[o], rt_send.at[o], rt_recv.at[o], (o, 0, 0))
        for o in range(1, outers)
    ]
    gather = [
        remote(gath.at[0, 0], gath.at[0, o], ag_send.at[o], ag_recv.at[o], (o, 0, 0))
        for o in range(1, outers)
    ]
    forward = [
        [
            remote(gath.at[0, o], gath.at[i, o], fw_send.at[i, o], fw_recv.at[i, o], (0, i, 0))
            for i in range(1, inners)
        ]
        for o in range(outers)
    ]
    for copy in scatter:
        copy.start()
    some = mine[inner].astype(jnp.float32)
    for i, copy in enumerate(scatter):
        copy.wait_recv()
        some = some + parts[i + 1].astype(jnp.float32)
    half[...] = some.astype(jnp.bfloat16)
    for copy in across:
        copy.start()
    own = half[outer].astype(jnp.float32)
    for o, copy in enumerate(across):
        copy.wait_recv()
        own = own + parts2[o + 1].astype(jnp.float32)
    gath[0, 0] = own.astype(jnp.bfloat16)
    for copy in gather + forward[0]:
        copy.start()
    load.wait()

    def correlate(i, o):
        j = lax.rem(outer - o + outers, outers) * inners + lax.rem(inner - i + inners, inners)
        sr = local_ref[j, 0].astype(jnp.float32)
        si = local_ref[j, 1].astype(jnp.float32)
        vr = gath[i, o, 0].astype(jnp.float32)
        vi = gath[i, o, 1].astype(jnp.float32)
        for s in range(nsrc):
            ar, ai = vr[s : s + 1], vi[s : s + 1]
            at = pl.ds(s * ch, ch)
            cross[at, :chunk] = (sr * ar + si * ai).astype(jnp.bfloat16)
            cross[at, chunk:] = (si * ar - sr * ai).astype(jnp.bfloat16)
        return jnp.dot(cross[...], table[j], preferred_element_type=jnp.float32)

    bounds = bounds_ref[...]
    at = lax.broadcasted_iota(jnp.int32, (nsrc, LAGS), 1).astype(jnp.float32)
    window[...] = (
        (at >= column(bounds[0:1])) & (at < column(bounds[1:2]))
    ).astype(jnp.float32)
    acc[...] = correlate(0, 0)
    for o in range(1, outers):
        gather[o - 1].wait_recv()
        for copy in forward[o]:
            copy.start()
    for o in range(1, outers):
        acc[...] += correlate(0, o)

    def step(o, carry):
        for i in range(1, inners):
            remote(
                gath.at[0, o], gath.at[i, o], fw_send.at[i, o], fw_recv.at[i, o], (0, i, 0)
            ).wait_recv()
            acc[...] += correlate(i, o)
        return carry

    lax.fori_loop(0, outers, step, 0)

    exchange = [
        remote(
            day_send.at[lax.rem(today + k, days)], day_recv.at[k], dy_send.at[k], dy_recv.at[k], (0, 0, k)
        )
        for k in range(1, days)
    ]
    for d in range(days):
        day_send[d] = acc[d * rows : (d + 1) * rows].astype(jnp.bfloat16)
    for copy in exchange:
        copy.start()

    lag = lax.broadcasted_iota(jnp.int32, (ch, LAGS), 1)
    member = (
        column(inter_ref[...]) == lax.broadcasted_iota(jnp.int32, (ch, LANES), 1).astype(jnp.float32)
    ).astype(jnp.float32)
    late = (
        column(inter_ref[...]) + LANES // 2
        == lax.broadcasted_iota(jnp.int32, (ch, LANES), 1).astype(jnp.float32)
    ).astype(jnp.float32)
    base = today * rows
    for copy in exchange:
        copy.wait_recv()
    nums = [jnp.zeros((ch, LAGS), jnp.float32) for _ in range(days)]
    dens = [jnp.zeros((ch, LAGS), jnp.float32) for _ in range(days)]
    for s in range(share):
        corrs = [acc[pl.ds(pl.multiple_of(base + s * ch, ch), ch)]]
        for k in range(1, days):
            corrs.append(day_recv[k, s * ch : (s + 1) * ch].astype(jnp.float32))
        mean = (sum(corrs[1:], corrs[0]) / days).astype(jnp.bfloat16)
        ref_out[s] = mean
        mean = mean.astype(jnp.float32)
        inside = window[pl.ds(today * share + s, 1)]
        for k in range(days):
            after = jnp.where(lag == LAGS - 1, 0.0, pltpu.roll(corrs[k], LAGS - 1, 1))
            before = jnp.where(lag == 0, 0.0, pltpu.roll(corrs[k], 1, 1))
            slope = 0.5 * (after - before)
            weighted = slope * inside
            nums[k] = nums[k] + weighted * (corrs[k] - mean)
            dens[k] = dens[k] + weighted * slope
    for k in range(days):
        num = jnp.sum(nums[k], axis=1, keepdims=True)
        den = jnp.sum(dens[k], axis=1, keepdims=True)
        fit[(days - k) % days] = jnp.sum(num * member + den * late, axis=0, keepdims=True)

    def landing(i, d):
        return days + d * inners + i

    plane = [
        remote(fit.at[d], fit.at[landing(i, d)], fp_send.at[i, d], fp_recv.at[i, d], (0, i, d))
        for d in range(days) for i in range(inners) if i or d
    ]
    for copy in plane:
        copy.start()
    total = fit[0]
    for copy in plane:
        copy.wait_recv()
    for d in range(days):
        for i in range(inners):
            if i or d:
                total = total + fit[landing(i, d)]
    held = days + days * inners
    fit[held] = total
    final = [
        remote(fit.at[held], fit.at[held + o], ft_send.at[o], ft_recv.at[o], (o, 0, 0))
        for o in range(1, outers)
    ]
    for copy in final:
        copy.start()
    for o, copy in enumerate(final):
        copy.wait_recv()
        total = total + fit[held + o + 1]
    drift_out[...] = (total / (pltpu.roll(total, LANES // 2, 1) + 1e-06))[:, :NINT]

    for copy in scatter + across + gather + sum(forward, []) + exchange + plane + final:
        copy.wait_send()


def per_device(n, days, spectra, source_index, interrogator, lag_bounds):
    _, ch, _, bins = spectra.shape
    nsrc = source_index.shape[0]
    chunk = bins // n
    share = nsrc // days
    inners = math.gcd(n, 4)
    outers = n // inners
    table = lag_table(bins, LAGS).reshape(2, n, chunk, LAGS).transpose(1, 0, 2, 3)
    table = jnp.asarray(table.reshape(n, 2 * chunk, LAGS))
    local = spectra[0].reshape(ch, 2, n, chunk).transpose(2, 1, 0, 3)
    vmem = pl.BlockSpec(memory_space=pltpu.VMEM)
    dma = pltpu.SemaphoreType.DMA
    bf16, f32 = jnp.bfloat16, jnp.float32
    ref_out, drift = pl.pallas_call(
        functools.partial(kernel, outers, inners, days),
        out_shape=(
            jax.ShapeDtypeStruct((share, ch, LAGS), bf16),
            jax.ShapeDtypeStruct((1, NINT), f32),
        ),
        in_specs=[
            pl.BlockSpec(memory_space=pl.ANY) for _ in range(5)
        ],
        out_specs=(vmem, vmem),
        scratch_shapes=[
            pltpu.VMEM((2, nsrc), jnp.int32),
            pltpu.VMEM((1, nsrc), jnp.int32),
            pltpu.VMEM((1, ch), jnp.int32),
            pltpu.VMEM((n, 2, ch, chunk), bf16),
            pltpu.VMEM((nsrc, LAGS), f32),
            pltpu.VMEM((n, 2 * chunk, LAGS), bf16),
            pltpu.VMEM((inners, outers, 2, nsrc, chunk), bf16),
            pltpu.VMEM((inners, outers, 2, nsrc, chunk), bf16),
            pltpu.VMEM((outers, 2, nsrc, chunk), bf16),
            pltpu.VMEM((outers, 2, nsrc, chunk), bf16),
            pltpu.VMEM((inners, outers, 2, nsrc, chunk), bf16),
            pltpu.VMEM((nsrc * ch, 2 * chunk), bf16),
            pltpu.VMEM((nsrc * ch, LAGS), f32),
            pltpu.VMEM((days, share * ch, LAGS), bf16),
            pltpu.VMEM((days, share * ch, LAGS), bf16),
            pltpu.VMEM((days + days * inners + outers, 1, LANES), f32),
            dma((4,)), dma, dma((inners,)), dma((inners,)), dma((outers,)), dma((outers,)),
            dma((outers,)), dma((outers,)), dma((inners, outers)), dma((inners, outers)),
            dma((days,)), dma((days,)), dma((inners, days)), dma((inners, days)),
            dma((outers,)), dma((outers,)),
        ],
        compiler_params=pltpu.CompilerParams(
            collective_id=0, has_side_effects=True, vmem_limit_bytes=60 * 1024 * 1024
        ),
    )(lag_bounds.T, source_index[None], interrogator[None], local, table)
    return ref_out, drift


def solution(mesh):
    return jax.shard_map(
        functools.partial(per_device, mesh.shape["chan"], mesh.shape["day"]),
        mesh=mesh,
        in_specs=(P("day", "chan", None, None), P(), P("chan"), P()),
        out_specs=(P("day", "chan", None), P("day", None)),
        check_vma=False,
    )
```

```python
import functools
import math

import jax
import jax.numpy as jnp
import numpy as np
from jax import lax
from jax.experimental import pallas as pl
from jax.experimental.pallas import tpu as pltpu
from jax.sharding import PartitionSpec as P

LAGS = 256
NINT = 8
LANES = 128
MESH = pl.DeviceIdType.MESH


def lag_table(bins, lags):
    freq = np.arange(bins, dtype=np.int32)
    shift = np.arange(lags, dtype=np.int32) - lags // 2
    phase = freq[:, None] * shift[None, :] % (2 * bins)
    angle = np.float32(math.pi) * phase.astype(np.float32) / np.float32(bins)
    scale = np.float32(1.0 / math.sqrt(bins))
    return np.stack([np.cos(angle) * scale, -np.sin(angle) * scale]).astype(jnp.bfloat16)


def column(row):
    m = row.shape[1]
    wide = jnp.broadcast_to(row.astype(jnp.float32), (m, m))
    eye = lax.broadcasted_iota(jnp.int32, (m, m), 0) == lax.broadcasted_iota(jnp.int32, (m, m), 1)
    return jnp.sum(jnp.where(eye, wide, 0.0), axis=1, keepdims=True)


def kernel(
    outers, inners, days, bounds_hbm, index_hbm, inter_hbm, local_hbm, table_hbm, ref_out, drift_out,
    bounds_ref, index_ref, inter_ref, local_ref, window, table, mine, parts, gath, cross, acc, day_send, day_recv, fit,
    in_sem, table_sem, rs_send, rs_recv, ag_send, ag_recv, fw_send, fw_recv,
    dy_send, dy_recv, fp_send, fp_recv, ft_send, ft_recv,
):
    n = outers * inners
    me = lax.axis_index("chan")
    outer, inner = me // inners, lax.rem(me, inners)
    today = lax.axis_index("day")
    ch = local_ref.shape[2]
    nsrc = mine.shape[3]
    chunk = mine.shape[4]
    share = nsrc // days
    rows = share * ch

    load = pltpu.make_async_copy(table_hbm, table, table_sem)
    ins = [
        pltpu.make_async_copy(src, dst, in_sem.at[i])
        for i, (src, dst) in enumerate([
            (index_hbm, index_ref), (local_hbm, local_ref),
            (inter_hbm, inter_ref), (bounds_hbm, bounds_ref),
        ])
    ]
    for copy in ins:
        copy.start()
    load.start()

    barrier = pltpu.get_barrier_semaphore()

    def along(o, i, d):
        chan = lax.rem(outer + o, outers) * inners + lax.rem(inner + i, inners)
        return {"chan": chan, "day": lax.rem(today + d, days)}

    others = [(o, i) for o in reversed(range(outers)) for i in range(inners) if o or i]
    partners = [(o, i, 0) for o, i in others]
    partners += [(0, i, d) for d in range(1, days) for i in range(inners)]
    for partner in partners:
        pl.semaphore_signal(barrier, inc=1, device_id=along(*partner), device_id_type=MESH)

    for copy in ins:
        copy.wait()

    wanted = column(index_ref[...]) - (me * ch).astype(jnp.float32)
    select = (
        wanted == lax.broadcasted_iota(jnp.int32, (nsrc, ch), 1).astype(jnp.float32)
    ).astype(jnp.bfloat16)

    for i in range(inners):
        for o in range(outers):
            for part in range(2):
                mine[i, o, part] = jnp.dot(
                    select, local_ref[o * inners + i, part], preferred_element_type=jnp.float32
                ).astype(jnp.bfloat16)
    pl.semaphore_wait(barrier, len(partners))

    def remote(src, dst, send_sem, recv_sem, to):
        return pltpu.make_async_remote_copy(
            src_ref=src, dst_ref=dst, send_sem=send_sem, recv_sem=recv_sem,
            device_id=along(*to), device_id_type=MESH,
        )

    scatter = [
        remote(
            mine.at[lax.rem(inner + i, inners), lax.rem(outer + o, outers)], parts.at[i, o],
            rs_send.at[i, o], rs_recv.at[i, o], (o, i, 0),
        )
        for o, i in others
    ]
    gather = [
        remote(gath.at[0, 0], gath.at[0, o], ag_send.at[o], ag_recv.at[o], (o, 0, 0))
        for o in range(1, outers)
    ]
    forward = [
        [
            remote(gath.at[0, o], gath.at[i, o], fw_send.at[i, o], fw_recv.at[i, o], (0, i, 0))
            for i in range(1, inners)
        ]
        for o in range(outers)
    ]
    for copy in scatter:
        copy.start()
    own = mine[inner, outer].astype(jnp.float32)
    for (o, i), copy in zip(others, scatter):
        copy.wait_recv()
        own = own + parts[i, o].astype(jnp.float32)
    gath[0, 0] = own.astype(jnp.bfloat16)
    for copy in gather + forward[0]:
        copy.start()
    load.wait()

    def correlate(i, o):
        j = lax.rem(outer - o + outers, outers) * inners + lax.rem(inner - i + inners, inners)
        sr = local_ref[j, 0].astype(jnp.float32)
        si = local_ref[j, 1].astype(jnp.float32)
        vr = gath[i, o, 0].astype(jnp.float32)
        vi = gath[i, o, 1].astype(jnp.float32)
        for s in range(nsrc):
            ar, ai = vr[s : s + 1], vi[s : s + 1]
            at = pl.ds(s * ch, ch)
            cross[at, :chunk] = (sr * ar + si * ai).astype(jnp.bfloat16)
            cross[at, chunk:] = (si * ar - sr * ai).astype(jnp.bfloat16)
        return jnp.dot(cross[...], table[j], preferred_element_type=jnp.float32)

    bounds = bounds_ref[...]
    at = lax.broadcasted_iota(jnp.int32, (nsrc, LAGS), 1).astype(jnp.float32)
    window[...] = (
        (at >= column(bounds[0:1])) & (at < column(bounds[1:2]))
    ).astype(jnp.float32)
    acc[...] = correlate(0, 0)
    for o in range(1, outers):
        gather[o - 1].wait_recv()
        for copy in forward[o]:
            copy.start()
    for o in range(1, outers):
        acc[...] += correlate(0, o)

    def step(o, carry):
        for i in range(1, inners):
            remote(
                gath.at[0, o], gath.at[i, o], fw_send.at[i, o], fw_recv.at[i, o], (0, i, 0)
            ).wait_recv()
            acc[...] += correlate(i, o)
        return carry

    lax.fori_loop(0, outers, step, 0)

    exchange = [
        remote(
            day_send.at[lax.rem(today + k, days)], day_recv.at[k], dy_send.at[k], dy_recv.at[k], (0, 0, k)
        )
        for k in range(1, days)
    ]
    for d in range(days):
        day_send[d] = acc[d * rows : (d + 1) * rows].astype(jnp.bfloat16)
    for copy in exchange:
        copy.start()

    lag = lax.broadcasted_iota(jnp.int32, (ch, LAGS), 1)
    member = (
        column(inter_ref[...]) == lax.broadcasted_iota(jnp.int32, (ch, LANES), 1).astype(jnp.float32)
    ).astype(jnp.float32)
    late = (
        column(inter_ref[...]) + LANES // 2
        == lax.broadcasted_iota(jnp.int32, (ch, LANES), 1).astype(jnp.float32)
    ).astype(jnp.float32)
    base = today * rows
    for copy in exchange:
        copy.wait_recv()
    nums = [jnp.zeros((ch, LAGS), jnp.float32) for _ in range(days)]
    dens = [jnp.zeros((ch, LAGS), jnp.float32) for _ in range(days)]
    for s in range(share):
        corrs = [acc[pl.ds(pl.multiple_of(base + s * ch, ch), ch)]]
        for k in range(1, days):
            corrs.append(day_recv[k, s * ch : (s + 1) * ch].astype(jnp.float32))
        mean = (sum(corrs[1:], corrs[0]) / days).astype(jnp.bfloat16)
        ref_out[s] = mean
        mean = mean.astype(jnp.float32)
        inside = window[pl.ds(today * share + s, 1)]
        for k in range(days):
            after = jnp.where(lag == LAGS - 1, 0.0, pltpu.roll(corrs[k], LAGS - 1, 1))
            before = jnp.where(lag == 0, 0.0, pltpu.roll(corrs[k], 1, 1))
            slope = 0.5 * (after - before)
            weighted = slope * inside
            nums[k] = nums[k] + weighted * (corrs[k] - mean)
            dens[k] = dens[k] + weighted * slope
    for k in range(days):
        num = jnp.sum(nums[k], axis=1, keepdims=True)
        den = jnp.sum(dens[k], axis=1, keepdims=True)
        fit[(days - k) % days] = jnp.sum(num * member + den * late, axis=0, keepdims=True)

    def landing(i, d):
        return days + d * inners + i

    plane = [
        remote(fit.at[d], fit.at[landing(i, d)], fp_send.at[i, d], fp_recv.at[i, d], (0, i, d))
        for d in range(days) for i in range(inners) if i or d
    ]
    for copy in plane:
        copy.start()
    total = fit[0]
    for copy in plane:
        copy.wait_recv()
    for d in range(days):
        for i in range(inners):
            if i or d:
                total = total + fit[landing(i, d)]
    held = days + days * inners
    fit[held] = total
    final = [
        remote(fit.at[held], fit.at[held + o], ft_send.at[o], ft_recv.at[o], (o, 0, 0))
        for o in range(1, outers)
    ]
    for copy in final:
        copy.start()
    for o, copy in enumerate(final):
        copy.wait_recv()
        total = total + fit[held + o + 1]
    drift_out[...] = (total / (pltpu.roll(total, LANES // 2, 1) + 1e-06))[:, :NINT]

    for copy in scatter + gather + sum(forward, []) + exchange + plane + final:
        copy.wait_send()


def per_device(n, days, spectra, source_index, interrogator, lag_bounds):
    _, ch, _, bins = spectra.shape
    nsrc = source_index.shape[0]
    chunk = bins // n
    share = nsrc // days
    inners = math.gcd(n, 4)
    outers = n // inners
    table = lag_table(bins, LAGS).reshape(2, n, chunk, LAGS).transpose(1, 0, 2, 3)
    table = jnp.asarray(table.reshape(n, 2 * chunk, LAGS))
    local = spectra[0].reshape(ch, 2, n, chunk).transpose(2, 1, 0, 3)
    vmem = pl.BlockSpec(memory_space=pltpu.VMEM)
    dma = pltpu.SemaphoreType.DMA
    bf16, f32 = jnp.bfloat16, jnp.float32
    ref_out, drift = pl.pallas_call(
        functools.partial(kernel, outers, inners, days),
        out_shape=(
            jax.ShapeDtypeStruct((share, ch, LAGS), bf16),
            jax.ShapeDtypeStruct((1, NINT), f32),
        ),
        in_specs=[
            pl.BlockSpec(memory_space=pl.ANY) for _ in range(5)
        ],
        out_specs=(vmem, vmem),
        scratch_shapes=[
            pltpu.VMEM((2, nsrc), jnp.int32),
            pltpu.VMEM((1, nsrc), jnp.int32),
            pltpu.VMEM((1, ch), jnp.int32),
            pltpu.VMEM((n, 2, ch, chunk), bf16),
            pltpu.VMEM((nsrc, LAGS), f32),
            pltpu.VMEM((n, 2 * chunk, LAGS), bf16),
            pltpu.VMEM((inners, outers, 2, nsrc, chunk), bf16),
            pltpu.VMEM((inners, outers, 2, nsrc, chunk), bf16),
            pltpu.VMEM((inners, outers, 2, nsrc, chunk), bf16),
            pltpu.VMEM((nsrc * ch, 2 * chunk), bf16),
            pltpu.VMEM((nsrc * ch, LAGS), f32),
            pltpu.VMEM((days, share * ch, LAGS), bf16),
            pltpu.VMEM((days, share * ch, LAGS), bf16),
            pltpu.VMEM((days + days * inners + outers, 1, LANES), f32),
            dma((4,)), dma, dma((inners, outers)), dma((inners, outers)),
            dma((outers,)), dma((outers,)), dma((inners, outers)), dma((inners, outers)),
            dma((days,)), dma((days,)), dma((inners, days)), dma((inners, days)),
            dma((outers,)), dma((outers,)),
        ],
        compiler_params=pltpu.CompilerParams(
            collective_id=0, has_side_effects=True, vmem_limit_bytes=60 * 1024 * 1024
        ),
    )(lag_bounds.T, source_index[None], interrogator[None], local, table)
    return ref_out, drift


def solution(mesh):
    return jax.shard_map(
        functools.partial(per_device, mesh.shape["chan"], mesh.shape["day"]),
        mesh=mesh,
        in_specs=(P("day", "chan", None, None), P(), P("chan"), P()),
        out_specs=(P("day", "chan", None), P("day", None)),
        check_vma=False,
    )
```
